32 devices in a mesh: groups: 2 (over y), space: 4 (over z), feat: 2 (over x), sub: 2 (over core).
Axes of the slice: x: 2, y: 2, z: 4, core: 2. Of those that a mesh axis runs over, the one named last changes fastest.
Arguments:
- x_grid: bfloat16 [2048, 227], P(('groups', 'space')), parts along dimension 0, may hold values from -6 to 6
- mesh_nodes: bfloat16 [1024, 512], P('space', 'feat'), may hold values from -6 to 6
- w_embed: bfloat16 [227, 512], P(None, 'feat'), may hold values from -0.375 to 0.375
- w_send: bfloat16 [3, 512, 512], P(None, None, 'feat'), may hold values from -0.25 to 0.25
- w_recv: bfloat16 [3, 512, 512], P(None, None, 'feat'), may hold values from -0.25 to 0.25
- w_out: bfloat16 [3, 512, 512], P(None, 'feat'), may hold values from -0.03125 to 0.03125
- edge_bias: float32 [3, 512], P(None, 'feat'), may hold values from -4 to 4
- enc_sources: int32 [128, 128], P(('space', 'sub')), may hold values from 0 to 255
- enc_owners: int32 [128, 1], P(('space', 'sub')), may hold values from 0 to 3; in each aligned block of 16 rows (0 to 15, 16 to 31, ...) at most 8 rows name the same one
- enc_blocks: int32 [128], P(('space', 'sub')), may hold values from 0 to 1
- enc_offsets: int32 [128, 128], P(('space', 'sub')), may hold values from -1 to 127
- proc_sources: int32 [128, 128], P(('space', 'sub')), may hold values from 0 to 255
- proc_owners: int32 [128, 1], P(('space', 'sub')), may hold values from 0 to 3; in each aligned block of 16 rows (0 to 15, 16 to 31, ...) at most 8 rows name the same one
- proc_blocks: int32 [128], P(('space', 'sub')), may hold values from 0 to 1
- proc_offsets: int32 [128, 128], P(('space', 'sub')), may hold values from -1 to 127
- dec_sources: int32 [128, 128], P(('space', 'sub')), may hold values from 0 to 255
- dec_owners: int32 [128, 1], P(('space', 'sub')), may hold values from 0 to 3; in each aligned block of 16 rows (0 to 15, 16 to 31, ...) at most 8 rows name the same one
- dec_blocks: int32 [128], P(('space', 'sub')), may hold values from 0 to 1
- dec_offsets: int32 [128, 128], P(('space', 'sub')), may hold values from -1 to 127
Outputs:
- grid_out: bfloat16 [2048, 512], P(('groups', 'space'), 'feat'), parts along dimension 0
The draws below stay inside these ranges and needn't reach their ends.
There are 2 independent parts, one for each index of `groups`. The reference program is written for one: setup_inputs(seed, part) draws one part's arguments, and reference() takes and returns one part's arrays. A program takes and returns all parts, laid end to end along the dimension named above; an argument that names none is the same for every part. Nothing has to cross between parts.
Inputs may be any that keep to these rules, and one draw needn't show every extreme that they name: `enc_owners`: among the 16 edge blocks of one device, no owner is named more than 8 times, a bound that some block reaches. `proc_owners`: as for enc_owners. `dec_owners`: as for enc_owners.
All inputs are finite; a program needn't handle non-finite values.
Results may differ from the reference program's by a relative error of at most 0.0055.
Values may be sent and summed in bfloat16 or wider, within the bound.
A program may use at most 64 MiB of HBM per device.

```python
import math
import jax
import jax.numpy as jnp
import numpy as np
from jax import lax

C_IN = 227
LAT = 512
HID = 512
GRID_DEV = 256
MESH_DEV = 256
BLK = 16
GRID = 1024
MESH = 1024
CAP = 8
EB = 128
N_SPACE = 4
N_SUB = 2


def with_ends(entries, own_key, smallest, top_value):
    extent = entries.shape
    spot = [jax.random.randint(jax.random.fold_in(own_key, axis), (), 0, extent[axis]) for axis in range(len(extent))]
    entries = entries.at[tuple(spot)].set(smallest)
    longest = extent.index(max(extent))
    spot[longest] = (spot[longest] + 1) % extent[longest]
    return entries.at[tuple(spot)].set(top_value)


def steps_of(key, shape, split, low, top_value):
    factor_of = 1.0
    for dim, blocks in split:
        steps = jax.random.uniform(jax.random.fold_in(jax.random.fold_in(key, 6), dim), (blocks,), jnp.float32, low / len(split), top_value / len(split))
        factor_of = factor_of * jnp.repeat(jnp.exp(steps), shape[dim] // blocks).reshape((-1,) + (1,) * (len(shape) - 1 - dim))
    return factor_of


def shared_out(rng, own, number, rows, amount, top, reach, skew):
    sequence = jax.random.permutation(rng, amount)
    packed, common = load_shares(amount, rows * top, reach, skew, True), load_shares(amount, rows * top, reach, skew, False)
    places = jnp.arange(amount)

    def named(lengths, rotation):
        used = int((lengths > 0).sum())
        fixed = max(1, used // 4)
        shifted = fixed + (places - fixed + rotation * (used - fixed)) % max(1, amount - fixed)
        return jnp.zeros((amount,), jnp.int32).at[sequence[jnp.where(places < fixed, places, shifted)]].set(jnp.asarray(lengths, jnp.int32))

    lengths = jnp.where(number % 4 == 0, named(packed, number // 4), named(common, number - number // 4 - 1))
    mixed = jax.random.permutation(jax.random.fold_in(own, 3), amount)
    giver, sink = mixed[0:amount // 2 * 2:2], mixed[1:amount // 2 * 2:2]
    margin = jnp.minimum(lengths[giver] - 1, reach - lengths[sink]) // 2
    margin = jnp.where((giver == sequence[0]) | (sink == sequence[0]) | (lengths[sink] == 0), 0, jnp.maximum(margin, 0))
    shifted = jax.random.randint(jax.random.fold_in(own, 4), (amount // 2,), 0, 1 << 20) % (margin + 1)
    lengths = lengths.at[giver].add(-shifted).at[sink].add(shifted)
    labels = jnp.searchsorted(jnp.cumsum(lengths), jnp.arange(rows * top), side="right").astype(jnp.int32)
    table = labels.reshape(top, rows).T
    table = table[jax.random.permutation(jax.random.fold_in(own, 1), rows)]
    rotation = jax.random.randint(jax.random.fold_in(own, 2), (rows, 1), 0, top)
    return jnp.take_along_axis(table, (jnp.arange(top)[None, :] + rotation) % top, axis=1)


def load_shares(amount, total, limit, skew, full):
    portions = [(1 << 20) // math.isqrt(grade ** skew) + 1 for grade in range(1, amount + 1)]
    largest = limit if full else min(limit, max(-(-total // amount), total * portions[0] // sum(portions)))
    least = 1 if total - largest >= amount - 1 else 0
    holding, spare = [largest] + [least] * (amount - 1), total - largest - least * (amount - 1)
    while spare > 0:
        movable = [i for i in range(1, amount) if holding[i] < largest] or [i for i in range(1, amount) if holding[i] < limit]
        whole, left = sum([portions[i] for i in movable]), spare
        for i in movable:
            addition = min(limit - holding[i], max(1, left * portions[i] // whole), spare)
            holding[i] = holding[i] + addition
            spare = spare - addition
    return np.array(holding)


def noise(key, dims, width, limit, pieces=(), kind=jnp.bfloat16):
    result = width * jax.random.normal(key, dims, jnp.float32)
    if pieces:
        result = result * steps_of(key, dims, pieces, -0.22, 0.18)
    return jnp.clip(result, -limit, limit).astype(kind)


def setup_inputs(seed: int = 0, part: int = 0) -> dict:
    splits = jax.random.split(jax.random.key(seed), 20)
    own_keys = jax.random.split(jax.random.fold_in(splits[19], part), 20)
    x_grid = noise(own_keys[0], (GRID, C_IN), 1.0, 6.0, ((0, 4),))
    mesh_nodes = noise(splits[1], (MESH, LAT), 1.0, 6.0, ((0, 4), (1, 2)))
    w_embed = noise(splits[2], (C_IN, LAT), C_IN ** -0.5, 0.375, ((1, 2),))
    w_send = noise(splits[3], (3, LAT, HID), LAT ** -0.5, 0.25, ((2, 2),))
    w_recv = noise(splits[4], (3, LAT, HID), LAT ** -0.5, 0.25, ((2, 2),))
    w_out = noise(splits[5], (3, HID, LAT), (HID * 64) ** -0.5, 0.03125, ((1, 2),))
    edge_bias = noise(splits[6], (3, HID), 1.0, 4.0, ((1, 2),), jnp.float32)
    enc_sources = with_ends(jax.random.randint(splits[7], (EB, 128), 0, GRID_DEV), jax.random.fold_in(splits[7], 1), 0, GRID_DEV - 1).astype(jnp.int32)
    enc_owners_keys = jax.random.split(jax.random.fold_in(splits[8], 1), EB // BLK)
    enc_owners_turns = jax.random.permutation(jax.random.fold_in(splits[8], 3), EB // BLK)
    enc_owners = jax.vmap(lambda own, number: shared_out(jax.random.fold_in(splits[8], 2), own, number, BLK, N_SPACE, 1, CAP, 2))(enc_owners_keys, enc_owners_turns).reshape((EB, 1))
    enc_blocks = with_ends(jax.random.randint(splits[9], (EB,), 0, MESH_DEV // 128), jax.random.fold_in(splits[9], 1), 0, (MESH_DEV // 128) - 1).astype(jnp.int32)
    enc_offsets = with_ends(jax.random.randint(splits[10], (EB, 128), -1, 128), jax.random.fold_in(splits[10], 1), -1, 127).astype(jnp.int32)
    proc_sources = with_ends(jax.random.randint(splits[11], (EB, 128), 0, MESH_DEV), jax.random.fold_in(splits[11], 1), 0, MESH_DEV - 1).astype(jnp.int32)
    proc_owners_keys = jax.random.split(jax.random.fold_in(splits[12], 1), EB // BLK)
    proc_owners_turns = jax.random.permutation(jax.random.fold_in(splits[12], 3), EB // BLK)
    proc_owners = jax.vmap(lambda own, number: shared_out(jax.random.fold_in(splits[12], 2), own, number, BLK, N_SPACE, 1, CAP, 1))(proc_owners_keys, proc_owners_turns).reshape((EB, 1))
    proc_blocks = with_ends(jax.random.randint(splits[13], (EB,), 0, MESH_DEV // 128), jax.random.fold_in(splits[13], 1), 0, (MESH_DEV // 128) - 1).astype(jnp.int32)
    proc_offsets = with_ends(jax.random.randint(splits[14], (EB, 128), -1, 128), jax.random.fold_in(splits[14], 1), -1, 127).astype(jnp.int32)
    dec_sources = with_ends(jax.random.randint(splits[15], (EB, 128), 0, MESH_DEV), jax.random.fold_in(splits[15], 1), 0, MESH_DEV - 1).astype(jnp.int32)
    dec_owners_keys = jax.random.split(jax.random.fold_in(splits[16], 1), EB // BLK)
    dec_owners_turns = jax.random.permutation(jax.random.fold_in(splits[16], 3), EB // BLK)
    dec_owners = jax.vmap(lambda own, number: shared_out(jax.random.fold_in(splits[16], 2), own, number, BLK, N_SPACE, 1, CAP, 2))(dec_owners_keys, dec_owners_turns).reshape((EB, 1))
    dec_blocks = with_ends(jax.random.randint(splits[17], (EB,), 0, GRID_DEV // 128), jax.random.fold_in(splits[17], 1), 0, (GRID_DEV // 128) - 1).astype(jnp.int32)
    dec_offsets = with_ends(jax.random.randint(splits[18], (EB, 128), -1, 128), jax.random.fold_in(splits[18], 1), -1, 127).astype(jnp.int32)
    return {"x_grid": x_grid, "mesh_nodes": mesh_nodes, "w_embed": w_embed, "w_send": w_send, "w_recv": w_recv, "w_out": w_out, "edge_bias": edge_bias, "enc_sources": enc_sources, "enc_owners": enc_owners, "enc_blocks": enc_blocks, "enc_offsets": enc_offsets, "proc_sources": proc_sources, "proc_owners": proc_owners, "proc_blocks": proc_blocks, "proc_offsets": proc_offsets, "dec_sources": dec_sources, "dec_owners": dec_owners, "dec_blocks": dec_blocks, "dec_offsets": dec_offsets}


def section(sender, receiver, w_s, w_r, w_o, hid_bias, sources, owners, blocks, offsets, send_rows, recv_rows):
    ps = jnp.dot(sender, w_s, preferred_element_type=jnp.float32).astype(jnp.bfloat16)
    pr = jnp.dot(receiver, w_r, preferred_element_type=jnp.float32).astype(jnp.bfloat16)
    block_count = sources.shape[0]
    device_row = jnp.arange(block_count, dtype=jnp.int32) // BLK
    space_row = device_row // N_SUB
    global_src = (space_row[:, None] * send_rows + sources).reshape(-1)
    present = offsets >= 0
    total_recv = receiver.shape[0]
    global_dst = owners[:, 0][:, None] * recv_rows + blocks[:, None] * 128 + jnp.maximum(offsets, 0)
    global_dst = jnp.where(present, global_dst, total_recv).reshape(-1).astype(jnp.int32)
    safe_dst = jnp.minimum(global_dst, total_recv - 1)
    value = ps[global_src].astype(jnp.float32) + pr[safe_dst].astype(jnp.float32) + hid_bias[None, :]
    hidden = jax.nn.silu(value).astype(jnp.bfloat16)
    agg = jax.ops.segment_sum(hidden.astype(jnp.float32), global_dst, num_segments=total_recv + 1)[:total_recv]
    update = jnp.dot(agg, w_o.astype(jnp.float32), precision=lax.Precision.HIGHEST)
    return (receiver.astype(jnp.float32) + update).astype(jnp.bfloat16)


def reference(x_grid, mesh_nodes, w_embed, w_send, w_recv, w_out, edge_bias,
              enc_sources, enc_owners, enc_blocks, enc_offsets,
              proc_sources, proc_owners, proc_blocks, proc_offsets,
              dec_sources, dec_owners, dec_blocks, dec_offsets):
    grid = jnp.dot(x_grid, w_embed, preferred_element_type=jnp.float32).astype(jnp.bfloat16)
    mesh_one = section(grid, mesh_nodes, w_send[0], w_recv[0], w_out[0], edge_bias[0],
                     enc_sources, enc_owners, enc_blocks, enc_offsets, GRID_DEV, MESH_DEV)
    mesh_two = section(mesh_one, mesh_one, w_send[1], w_recv[1], w_out[1], edge_bias[1],
                     proc_sources, proc_owners, proc_blocks, proc_offsets, MESH_DEV, MESH_DEV)
    return section(mesh_two, grid, w_send[2], w_recv[2], w_out[2], edge_bias[2],
                 dec_sources, dec_owners, dec_blocks, dec_offsets, MESH_DEV, GRID_DEV)
```

```python
import functools

import jax
import jax.numpy as jnp
from jax import lax
from jax.experimental import pallas as pl
from jax.experimental.pallas import tpu as pltpu
from jax.sharding import PartitionSpec as P


def make_hidden(send_part, recv_part, offsets, bias_cols):
    value = send_part.astype(jnp.float32) + recv_part.astype(jnp.float32) + bias_cols
    hidden = jax.nn.silu(value)
    return jnp.where((offsets >= 0)[..., None], hidden, 0.0).astype(jnp.bfloat16)


def block_sum(hidden, offsets, block_ids, block_total):
    node_hot = (offsets[:, :, None] == jnp.arange(128, dtype=jnp.int32)[None, None, :]).astype(
        jnp.bfloat16
    )
    per_block = jnp.einsum("nep,nec->npc", node_hot, hidden, preferred_element_type=jnp.float32)
    block_hot = (block_ids[:, None] == jnp.arange(block_total, dtype=jnp.int32)[None, :]).astype(
        jnp.float32
    )
    summed = jnp.einsum("nb,npc->bpc", block_hot, per_block, precision=lax.Precision.HIGHEST)
    return summed.reshape(block_total * 128, hidden.shape[2])


def section(
    sender,
    receiver,
    section_index,
    w_send,
    w_recv,
    w_out,
    edge_bias,
    sources,
    owners,
    blocks,
    offsets,
):
    send_weight = w_send[section_index]
    recv_weight = w_recv[section_index]
    bias_cols = edge_bias[section_index]
    send_proj = jnp.dot(
        lax.all_gather(sender, "feat", axis=1, tiled=True),
        send_weight,
        preferred_element_type=jnp.float32,
    )
    recv_proj = jnp.dot(
        lax.all_gather(receiver, "feat", axis=1, tiled=True),
        recv_weight,
        preferred_element_type=jnp.float32,
    )
    send_proj = send_proj.astype(jnp.bfloat16)
    recv_proj = recv_proj.astype(jnp.bfloat16)
    recv_count = receiver.shape[0]
    recv_blocks = recv_count // 128
    owner_ids = owners[:, 0]
    space_count = lax.axis_size("space")
    block_count = sources.shape[0]
    capacity = max(2, 2 * block_count // space_count)
    slot_count = space_count * capacity
    owner_hot = (owner_ids[:, None] == jnp.arange(space_count, dtype=jnp.int32)[None, :]).astype(
        jnp.int32
    )
    place_rank = jnp.sum((jnp.cumsum(owner_hot, axis=0) - owner_hot) * owner_hot, axis=1)
    slot_of_block = owner_ids * capacity + place_rank
    slot_match = slot_of_block[None, :] == jnp.arange(slot_count, dtype=jnp.int32)[:, None]
    occupied = jnp.any(slot_match, axis=1)
    block_pick = jnp.sum(
        jnp.where(slot_match, jnp.arange(block_count, dtype=jnp.int32)[None, :], 0), axis=1
    )
    sent_offsets = jnp.where(occupied[:, None], offsets[block_pick], -1)
    sent_blocks = blocks[block_pick]
    send_rows = send_proj[sources[block_pick]]
    sent_data = jnp.where(occupied[:, None, None], send_rows, jnp.zeros_like(send_rows))
    arrived, arrived_offsets, arrived_blocks = (
        lax.all_to_all(sent_data, "space", split_axis=0, concat_axis=0, tiled=True),
        lax.all_to_all(sent_offsets, "space", split_axis=0, concat_axis=0, tiled=True),
        lax.all_to_all(sent_blocks, "space", split_axis=0, concat_axis=0, tiled=True),
    )
    target_rows = arrived_blocks[:, None] * 128 + jnp.maximum(arrived_offsets, 0)
    hidden = make_hidden(arrived, recv_proj[target_rows], arrived_offsets, bias_cols)
    edge_sums = block_sum(hidden, arrived_offsets, arrived_blocks, recv_blocks)
    edge_sums = lax.psum(edge_sums, "sub")
    out_rows = w_out[section_index].astype(jnp.float32)
    partial_update = jnp.dot(edge_sums, out_rows, precision=lax.Precision.HIGHEST)
    update = lax.psum_scatter(partial_update, "feat", scatter_dimension=1, tiled=True)
    return (receiver.astype(jnp.float32) + update).astype(jnp.bfloat16)


def on_device(
    x_grid,
    mesh_nodes,
    w_embed,
    w_send,
    w_recv,
    w_out,
    edge_bias,
    enc_sources,
    enc_owners,
    enc_blocks,
    enc_offsets,
    proc_sources,
    proc_owners,
    proc_blocks,
    proc_offsets,
    dec_sources,
    dec_owners,
    dec_blocks,
    dec_offsets,
):
    grid = jnp.dot(x_grid, w_embed, preferred_element_type=jnp.float32).astype(jnp.bfloat16)
    mesh_one = section(
        grid,
        mesh_nodes,
        0,
        w_send,
        w_recv,
        w_out,
        edge_bias,
        enc_sources,
        enc_owners,
        enc_blocks,
        enc_offsets,
    )
    mesh_two = section(
        mesh_one,
        mesh_one,
        1,
        w_send,
        w_recv,
        w_out,
        edge_bias,
        proc_sources,
        proc_owners,
        proc_blocks,
        proc_offsets,
    )
    return section(
        mesh_two,
        grid,
        2,
        w_send,
        w_recv,
        w_out,
        edge_bias,
        dec_sources,
        dec_owners,
        dec_blocks,
        dec_offsets,
    )


MESH = pl.DeviceIdType.MESH
LANES = 128
CAP = 8
CHUNK = 4
F32 = jnp.float32
BF16 = jnp.bfloat16


def fits_kernel(mesh):
    sizes = mesh.shape
    return sizes["feat"] == 2 and sizes["sub"] == 2 and sizes["space"] == 4


def partner(me, k):
    result, bit = me, 1
    while bit <= k:
        if k & bit:
            result = result + bit - 2 * bit * lax.rem(lax.div(me, bit), 2)
        bit *= 2
    return result


def mm(a, b):
    return jnp.dot(a, b, preferred_element_type=F32)


def fused_kernel(
    n_space,
    x_ref,
    mesh_ref,
    w_embed_ref,
    w_send_ref,
    w_recv_ref,
    w_out_ref,
    bias_ref,
    small_ref,
    small_row_ref,
    src0_ref,
    off0_ref,
    src1_ref,
    off1_ref,
    src2_ref,
    off2_ref,
    out_ref,
    grid_full,
    mesh_full,
    latent,
    meta_send,
    meta_buf,
    ps_buf,
    pr_buf,
    agg_buf,
    wout_peer,
    wout_last,
    bias_buf,
    hots,
    meta_ss,
    meta_rs,
    feat_ss,
    feat_rs,
    ps_ss,
    ps_rs,
    agg_ss,
    agg_rs,
):
    s_me = lax.axis_index("space")
    f_me = lax.axis_index("feat")
    u_me = lax.axis_index("sub")
    f_other, u_other = 1 - f_me, 1 - u_me
    sends = []

    def remote(src, dst, send_sem, recv_sem, space=None, feat=None, sub=None):
        return pltpu.make_async_remote_copy(
            src_ref=src,
            dst_ref=dst,
            send_sem=send_sem,
            recv_sem=recv_sem,
            device_id={
                "space": s_me if space is None else space,
                "feat": f_me if feat is None else feat,
                "sub": u_me if sub is None else sub,
            },
            device_id_type=MESH,
        )

    def push(*args, **kwargs):
        copy = remote(*args, **kwargs)
        copy.start()
        sends.append(copy)

    meta_peers = [
        (partner(s_me, k), u_other if flip else u_me)
        for k in range(n_space)
        for flip in (0, 1)
        if k or flip
    ]
    quad_peers = [(f_me, u_other), (f_other, u_me), (f_other, u_other)]

    barrier = pltpu.get_barrier_semaphore()
    for space, sub in meta_peers:
        pl.semaphore_signal(
            barrier,
            inc=1,
            device_id={"space": space, "feat": f_me, "sub": sub},
            device_id_type=MESH,
        )
    for feat, sub in quad_peers[1:]:
        pl.semaphore_signal(
            barrier,
            inc=1,
            device_id={"space": s_me, "feat": feat, "sub": sub},
            device_id_type=MESH,
        )

    grid_full[f_me] = mm(x_ref[...], w_embed_ref[...]).astype(BF16)
    mesh_full[f_me] = mesh_ref[...]

    block_count = small_ref.shape[0]
    slot_count = n_space * CAP
    before = lax.broadcasted_iota(jnp.int32, (block_count, block_count), 0) < lax.broadcasted_iota(
        jnp.int32, (block_count, block_count), 1
    )
    for t, (src_ref, off_ref) in enumerate(
        ((src0_ref, off0_ref), (src1_ref, off1_ref), (src2_ref, off2_ref))
    ):
        own_col = small_ref[:, 2 * t : 2 * t + 1]
        block_col = small_ref[:, 2 * t + 1 : 2 * t + 2]
        own_row = small_row_ref[2 * t : 2 * t + 1, :]
        earlier = jnp.where((own_col == own_row) & before, 1.0, 0.0)
        rank = jnp.sum(earlier, axis=0, keepdims=True)
        slot_row = own_row.astype(F32) * float(CAP) + rank
        slots = lax.broadcasted_iota(jnp.int32, (slot_count, block_count), 0).astype(F32)
        pick = jnp.where(slots == slot_row, 1.0, 0.0).astype(BF16)
        offs = off_ref[...]
        rows = jnp.where(offs >= 0, offs + 128 * block_col + 1, 0).astype(F32).astype(BF16)
        src_slots = mm(pick, src_ref[...].astype(F32).astype(BF16))
        row_slots = mm(pick, rows)
        for o in range(n_space):
            part = slice(o * CAP, (o + 1) * CAP)
            meta_send[o, t] = jnp.concatenate([src_slots[part], row_slots[part]], axis=0).astype(
                BF16
            )
    my_slot = s_me * 2 + u_me
    meta_buf[my_slot] = meta_send[s_me]

    pl.semaphore_wait(barrier, len(meta_peers) + 2)

    def feat_copy(index, src, dst):
        return remote(src, dst, feat_ss.at[index], feat_rs.at[index], feat=f_other)

    def feat_push(index, src, dst):
        copy = feat_copy(index, src, dst)
        copy.start()
        sends.append(copy)

    feat_push(0, grid_full.at[f_me], grid_full.at[f_me])
    for i, (space, sub) in enumerate(meta_peers):
        push(
            meta_send.at[space],
            meta_buf.at[my_slot],
            meta_ss.at[i],
            meta_rs.at[my_slot],
            space=space,
            sub=sub,
        )
    feat_push(1, mesh_ref, mesh_full.at[f_me])
    feat_push(2, w_out_ref.at[0], wout_peer.at[0])

    hid_cols = pl.ds(pl.multiple_of(u_me * LANES, LANES), LANES)
    for t in range(3):
        row = bias_ref[t : t + 1, hid_cols]
        bias_buf[t] = jnp.transpose(jnp.broadcast_to(row, (LANES, LANES)))

    def project(latents, weight_ref, t):
        width = latents.shape[2]
        total = mm(latents[0], weight_ref[t, 0:width, hid_cols])
        total += mm(latents[1], weight_ref[t, width : 2 * width, hid_cols])
        return jnp.transpose(total).astype(BF16)

    def start_ps(latents, t):
        ps_buf[t, s_me] = project(latents, w_send_ref, t)
        for k in range(1, n_space):
            push(
                ps_buf.at[t, s_me],
                ps_buf.at[t, s_me],
                ps_ss.at[t, k],
                ps_rs.at[t, s_me],
                space=partner(s_me, k),
            )

    rows_count = mesh_ref.shape[0]

    def build_hots(t):
        node = lax.broadcasted_iota(jnp.int32, (rows_count, LANES), 0).astype(F32)

        def body(i, carry):
            meta = meta_buf[i, t].astype(F32)
            for j in range(CAP):
                lanes = slice((j % CHUNK) * LANES, (j % CHUNK + 1) * LANES)
                place = i * (CAP // CHUNK) + j // CHUNK
                hots[t, place, 0:rows_count, lanes] = jnp.where(
                    node == meta[j : j + 1], 1.0, 0.0
                ).astype(BF16)
                hots[t, place, rows_count : 2 * rows_count, lanes] = jnp.where(
                    node + 1.0 == meta[CAP + j : CAP + j + 1], 1.0, 0.0
                ).astype(BF16)
            return carry

        lax.fori_loop(0, 2 * n_space, body, 0)

    def edges(t):
        per_space = 2 * CAP // CHUNK
        recv_table = pr_buf[t]
        bias = jnp.concatenate([bias_buf[t]] * CHUNK, axis=1)
        total = jnp.zeros((rows_count, LANES), F32)
        for k in range(n_space):
            space = partner(s_me, k)
            if k:
                remote(
                    ps_buf.at[t, space],
                    ps_buf.at[t, space],
                    ps_ss.at[t, k],
                    ps_rs.at[t, space],
                    space=space,
                ).wait_recv()
            send_table = ps_buf[t, space]

            def body(c, acc, send_table=send_table, space=space):
                place = space * per_space + c
                send_hot = hots[t, place, 0:rows_count, :]
                recv_hot = hots[t, place, rows_count : 2 * rows_count, :]
                half = 0.5 * (mm(send_table, send_hot) + mm(recv_table, recv_hot) + bias)
                hidden = (half + half * jnp.tanh(half)).astype(BF16)
                return acc + lax.dot_general(
                    recv_hot, hidden, (((1,), (1,)), ((), ())), preferred_element_type=F32
                )

            total = lax.fori_loop(0, per_space, body, total)
        return total

    q_me = f_me * 2 + u_me

    def start_agg(t, total):
        agg_buf[t, q_me] = total.astype(BF16)
        for i, (feat, sub) in enumerate(quad_peers):
            push(
                agg_buf.at[t, q_me],
                agg_buf.at[t, q_me],
                agg_ss.at[t, i],
                agg_rs.at[t, q_me],
                feat=feat,
                sub=sub,
            )

    def wait_agg(t):
        for i, (feat, sub) in enumerate(quad_peers):
            q = feat * 2 + sub
            remote(
                agg_buf.at[t, q],
                agg_buf.at[t, q],
                agg_ss.at[t, i],
                agg_rs.at[t, q],
                feat=feat,
                sub=sub,
            ).wait_recv()
        own = jnp.concatenate([agg_buf[t, f_me * 2], agg_buf[t, f_me * 2 + 1]], axis=1)
        other = jnp.concatenate([agg_buf[t, f_other * 2], agg_buf[t, f_other * 2 + 1]], axis=1)
        return own, other

    def advance(base, t, to):
        own, other = wait_agg(t)
        feat_copy(2 + t, w_out_ref.at[t], wout_peer.at[t]).wait_recv()
        width = base.shape[2]
        for f in range(2):
            cols = slice(f * width, (f + 1) * width)
            update = mm(own, w_out_ref[t, :, cols]) + mm(other, wout_peer[t, :, cols])
            latent[to, f] = (base[f].astype(F32) + update).astype(BF16)

    for i, (space, sub) in enumerate(meta_peers):
        slot = space * 2 + sub
        remote(
            meta_send.at[space],
            meta_buf.at[slot],
            meta_ss.at[i],
            meta_rs.at[slot],
            space=space,
            sub=sub,
        ).wait_recv()
    feat_copy(0, grid_full.at[f_other], grid_full.at[f_other]).wait_recv()
    start_ps(grid_full, 0)
    build_hots(0)
    feat_copy(1, mesh_ref, mesh_full.at[f_other]).wait_recv()
    pr_buf[0] = project(mesh_full, w_recv_ref, 0)
    start_agg(0, edges(0))
    build_hots(1)
    advance(mesh_full, 0, 0)

    feat_push(3, w_out_ref.at[1], wout_peer.at[1])
    start_ps(latent.at[0], 1)
    pr_buf[1] = project(latent.at[0], w_recv_ref, 1)
    pr_buf[2] = project(grid_full, w_recv_ref, 2)
    start_agg(1, edges(1))
    build_hots(2)
    advance(latent.at[0], 1, 1)

    half_width = out_ref.shape[1]
    their_cols = pl.ds(pl.multiple_of(f_other * half_width, LANES), half_width)
    my_cols = pl.ds(pl.multiple_of(f_me * half_width, LANES), half_width)
    feat_push(4, w_out_ref.at[2, :, their_cols], wout_last)
    start_ps(latent.at[1], 2)
    start_agg(2, edges(2))
    own, other = wait_agg(2)
    feat_copy(4, w_out_ref.at[2, :, their_cols], wout_last).wait_recv()
    update = mm(own, w_out_ref[2, :, my_cols]) + mm(other, wout_last[...])
    out_ref[...] = (grid_full[f_me].astype(F32) + update).astype(BF16)
    for copy in sends:
        copy.wait_send()


def fused_on_device(
    n_space,
    x_grid,
    mesh_nodes,
    w_embed,
    w_send,
    w_recv,
    w_out,
    edge_bias,
    enc_sources,
    enc_owners,
    enc_blocks,
    enc_offsets,
    proc_sources,
    proc_owners,
    proc_blocks,
    proc_offsets,
    dec_sources,
    dec_owners,
    dec_blocks,
    dec_offsets,
):
    small = jnp.concatenate(
        [
            enc_owners,
            enc_blocks[:, None],
            proc_owners,
            proc_blocks[:, None],
            dec_owners,
            dec_blocks[:, None],
        ],
        axis=1,
    )
    rows, half = mesh_nodes.shape
    lat = w_out.shape[2]
    vmem = pl.BlockSpec(memory_space=pltpu.VMEM)
    chunks = n_space * 2 * CAP // CHUNK
    dma = pltpu.SemaphoreType.DMA
    return pl.pallas_call(
        functools.partial(fused_kernel, n_space),
        out_shape=jax.ShapeDtypeStruct((rows, half), BF16),
        in_specs=[vmem] * 15,
        out_specs=vmem,
        scratch_shapes=[
            pltpu.VMEM((2, rows, half), BF16),
            pltpu.VMEM((2, rows, half), BF16),
            pltpu.VMEM((2, 2, rows, half), BF16),
            pltpu.VMEM((n_space, 3, 2 * CAP, LANES), BF16),
            pltpu.VMEM((2 * n_space, 3, 2 * CAP, LANES), BF16),
            pltpu.VMEM((3, n_space, LANES, rows), BF16),
            pltpu.VMEM((3, LANES, rows), BF16),
            pltpu.VMEM((3, 4, rows, LANES), BF16),
            pltpu.VMEM((2, half, lat), BF16),
            pltpu.VMEM((half, half), BF16),
            pltpu.VMEM((3, LANES, LANES), F32),
            pltpu.VMEM((3, chunks, 2 * rows, CHUNK * LANES), BF16),
            dma((2 * n_space,)),
            dma((2 * n_space,)),
            dma((5,)),
            dma((5,)),
            dma((3, n_space)),
            dma((3, n_space)),
            dma((3, 3)),
            dma((3, 4)),
        ],
        compiler_params=pltpu.CompilerParams(
            collective_id=0, has_side_effects=True, vmem_limit_bytes=52 * 1024 * 1024
        ),
    )(
        x_grid,
        mesh_nodes,
        w_embed,
        w_send,
        w_recv,
        w_out,
        edge_bias,
        small,
        small.T,
        enc_sources,
        enc_offsets,
        proc_sources,
        proc_offsets,
        dec_sources,
        dec_offsets,
    )


def solution(mesh):
    in_specs = (
        P(("groups", "space"), None),
        P("space", "feat"),
        P(None, "feat"),
        P(None, None, "feat"),
        P(None, None, "feat"),
        P(None, "feat", None),
        P(None, "feat"),
        P(("space", "sub"), None),
        P(("space", "sub"), None),
        P(("space", "sub")),
        P(("space", "sub"), None),
        P(("space", "sub"), None),
        P(("space", "sub"), None),
        P(("space", "sub")),
        P(("space", "sub"), None),
        P(("space", "sub"), None),
        P(("space", "sub"), None),
        P(("space", "sub")),
        P(("space", "sub"), None),
    )
    out_specs = P(("groups", "space"), "feat")
    run = on_device
    if fits_kernel(mesh):
        run = functools.partial(fused_on_device, mesh.shape["space"])
    return jax.shard_map(
        run, mesh=mesh, in_specs=in_specs, out_specs=out_specs, check_vma=False
    )
```

```python
import functools

import jax
import jax.numpy as jnp
from jax import lax
from jax.experimental import pallas as pl
from jax.experimental.pallas import tpu as pltpu
from jax.sharding import PartitionSpec as P


def make_hidden(send_part, recv_part, offsets, bias_cols):
    value = send_part.astype(jnp.float32) + recv_part.astype(jnp.float32) + bias_cols
    hidden = jax.nn.silu(value)
    return jnp.where((offsets >= 0)[..., None], hidden, 0.0).astype(jnp.bfloat16)


def block_sum(hidden, offsets, block_ids, block_total):
    node_hot = (offsets[:, :, None] == jnp.arange(128, dtype=jnp.int32)[None, None, :]).astype(
        jnp.bfloat16
    )
    per_block = jnp.einsum("nep,nec->npc", node_hot, hidden, preferred_element_type=jnp.float32)
    block_hot = (block_ids[:, None] == jnp.arange(block_total, dtype=jnp.int32)[None, :]).astype(
        jnp.float32
    )
    summed = jnp.einsum("nb,npc->bpc", block_hot, per_block, precision=lax.Precision.HIGHEST)
    return summed.reshape(block_total * 128, hidden.shape[2])


def section(
    sender,
    receiver,
    section_index,
    w_send,
    w_recv,
    w_out,
    edge_bias,
    sources,
    owners,
    blocks,
    offsets,
):
    send_weight = w_send[section_index]
    recv_weight = w_recv[section_index]
    bias_cols = edge_bias[section_index]
    send_proj = jnp.dot(
        lax.all_gather(sender, "feat", axis=1, tiled=True),
        send_weight,
        preferred_element_type=jnp.float32,
    )
    recv_proj = jnp.dot(
        lax.all_gather(receiver, "feat", axis=1, tiled=True),
        recv_weight,
        preferred_element_type=jnp.float32,
    )
    send_proj = send_proj.astype(jnp.bfloat16)
    recv_proj = recv_proj.astype(jnp.bfloat16)
    recv_count = receiver.shape[0]
    recv_blocks = recv_count // 128
    owner_ids = owners[:, 0]
    space_count = lax.axis_size("space")
    block_count = sources.shape[0]
    capacity = max(2, 2 * block_count // space_count)
    slot_count = space_count * capacity
    owner_hot = (owner_ids[:, None] == jnp.arange(space_count, dtype=jnp.int32)[None, :]).astype(
        jnp.int32
    )
    place_rank = jnp.sum((jnp.cumsum(owner_hot, axis=0) - owner_hot) * owner_hot, axis=1)
    slot_of_block = owner_ids * capacity + place_rank
    slot_match = slot_of_block[None, :] == jnp.arange(slot_count, dtype=jnp.int32)[:, None]
    occupied = jnp.any(slot_match, axis=1)
    block_pick = jnp.sum(
        jnp.where(slot_match, jnp.arange(block_count, dtype=jnp.int32)[None, :], 0), axis=1
    )
    sent_offsets = jnp.where(occupied[:, None], offsets[block_pick], -1)
    sent_blocks = blocks[block_pick]
    send_rows = send_proj[sources[block_pick]]
    sent_data = jnp.where(occupied[:, None, None], send_rows, jnp.zeros_like(send_rows))
    arrived, arrived_offsets, arrived_blocks = (
        lax.all_to_all(sent_data, "space", split_axis=0, concat_axis=0, tiled=True),
        lax.all_to_all(sent_offsets, "space", split_axis=0, concat_axis=0, tiled=True),
        lax.all_to_all(sent_blocks, "space", split_axis=0, concat_axis=0, tiled=True),
    )
    target_rows = arrived_blocks[:, None] * 128 + jnp.maximum(arrived_offsets, 0)
    hidden = make_hidden(arrived, recv_proj[target_rows], arrived_offsets, bias_cols)
    edge_sums = block_sum(hidden, arrived_offsets, arrived_blocks, recv_blocks)
    edge_sums = lax.psum(edge_sums, "sub")
    out_rows = w_out[section_index].astype(jnp.float32)
    partial_update = jnp.dot(edge_sums, out_rows, precision=lax.Precision.HIGHEST)
    update = lax.psum_scatter(partial_update, "feat", scatter_dimension=1, tiled=True)
    return (receiver.astype(jnp.float32) + update).astype(jnp.bfloat16)


def on_device(
    x_grid,
    mesh_nodes,
    w_embed,
    w_send,
    w_recv,
    w_out,
    edge_bias,
    enc_sources,
    enc_owners,
    enc_blocks,
    enc_offsets,
    proc_sources,
    proc_owners,
    proc_blocks,
    proc_offsets,
    dec_sources,
    dec_owners,
    dec_blocks,
    dec_offsets,
):
    grid = jnp.dot(x_grid, w_embed, preferred_element_type=jnp.float32).astype(jnp.bfloat16)
    mesh_one = section(
        grid,
        mesh_nodes,
        0,
        w_send,
        w_recv,
        w_out,
        edge_bias,
        enc_sources,
        enc_owners,
        enc_blocks,
        enc_offsets,
    )
    mesh_two = section(
        mesh_one,
        mesh_one,
        1,
        w_send,
        w_recv,
        w_out,
        edge_bias,
        proc_sources,
        proc_owners,
        proc_blocks,
        proc_offsets,
    )
    return section(
        mesh_two,
        grid,
        2,
        w_send,
        w_recv,
        w_out,
        edge_bias,
        dec_sources,
        dec_owners,
        dec_blocks,
        dec_offsets,
    )


MESH = pl.DeviceIdType.MESH
LANES = 128
CAP = 8
CHUNK = 4
F32 = jnp.float32
BF16 = jnp.bfloat16


def fits_kernel(mesh):
    sizes = mesh.shape
    return sizes["feat"] == 2 and sizes["sub"] == 2 and sizes["space"] == 4


def partner(me, k):
    result, bit = me, 1
    while bit <= k:
        if k & bit:
            result = result + bit - 2 * bit * lax.rem(lax.div(me, bit), 2)
        bit *= 2
    return result


def mm(a, b):
    return jnp.dot(a, b, preferred_element_type=F32)


def fused_kernel(
    n_space,
    x_hbm,
    mesh_hbm,
    w_embed_hbm,
    w_send_hbm,
    w_recv_hbm,
    w_out_hbm,
    bias_hbm,
    *rest,
):
    edge_hbm, rest = rest[:12], rest[12:]
    fused_body(
        n_space,
        x_hbm,
        mesh_hbm,
        w_embed_hbm,
        w_send_hbm,
        w_recv_hbm,
        w_out_hbm,
        bias_hbm,
        edge_hbm,
        *rest,
    )


def fused_body(
    n_space,
    x_hbm,
    mesh_hbm,
    w_embed_hbm,
    w_send_hbm,
    w_recv_hbm,
    w_out_hbm,
    bias_hbm,
    edge_hbm,
    out_ref,
    x_ref,
    w_embed_ref,
    w_send_ref,
    w_recv_ref,
    w_out_ref,
    bias_ref,
    src_ref,
    off_ref,
    owner_ref,
    block_ref,
    fetch_sem,
    sib_ss,
    sib_rs,
    grid_full,
    mesh_full,
    latent,
    meta_send,
    meta_buf,
    ps_buf,
    pr_buf,
    agg_buf,
    wout_peer,
    wout_last,
    bias_buf,
    hots,
    meta_ss,
    meta_rs,
    feat_ss,
    feat_rs,
    ps_ss,
    ps_rs,
    agg_ss,
    agg_rs,
):
    s_me = lax.axis_index("space")
    f_me = lax.axis_index("feat")
    u_me = lax.axis_index("sub")
    f_other, u_other = 1 - f_me, 1 - u_me
    sends = []
    fetched = {}
    hid_cols = pl.ds(pl.multiple_of(u_me * LANES, LANES), LANES)
    rows_count, half_width = mesh_hbm.shape
    piece_rows = rows_count // 2
    my_rows = pl.ds(pl.multiple_of(u_me * piece_rows, piece_rows), piece_rows)
    sib_rows = pl.ds(pl.multiple_of(u_other * piece_rows, piece_rows), piece_rows)
    wout_rows = half_width // 2
    my_wout = pl.ds(pl.multiple_of(u_me * wout_rows, wout_rows), wout_rows)
    sib_wout = pl.ds(pl.multiple_of(u_other * wout_rows, wout_rows), wout_rows)

    def fetch(name, src, dst):
        copy = pltpu.make_async_copy(src, dst, fetch_sem.at[len(fetched)])
        copy.start()
        fetched[name] = copy

    fetch("x", x_hbm, x_ref)
    fetch("w_embed", w_embed_hbm, w_embed_ref)
    for t in range(3):
        fetch(("owner", t), edge_hbm[4 * t], owner_ref.at[t])
        fetch(("block", t), edge_hbm[4 * t + 1], block_ref.at[t])
        fetch(("src", t), edge_hbm[4 * t + 2], src_ref.at[t])
        fetch(("off", t), edge_hbm[4 * t + 3], off_ref.at[t])
    fetch("mesh", mesh_hbm, mesh_full.at[f_me])
    fetch("w_send", w_send_hbm.at[:, :, hid_cols], w_send_ref)
    fetch("w_recv", w_recv_hbm.at[:, :, hid_cols], w_recv_ref)
    fetch("bias", bias_hbm.at[:, hid_cols], bias_ref)
    fetch("w_out", w_out_hbm, w_out_ref)

    def remote(src, dst, send_sem, recv_sem, space=None, feat=None, sub=None):
        return pltpu.make_async_remote_copy(
            src_ref=src,
            dst_ref=dst,
            send_sem=send_sem,
            recv_sem=recv_sem,
            device_id={
                "space": s_me if space is None else space,
                "feat": f_me if feat is None else feat,
                "sub": u_me if sub is None else sub,
            },
            device_id_type=MESH,
        )

    def push(*args, **kwargs):
        copy = remote(*args, **kwargs)
        copy.start()
        sends.append(copy)

    meta_peers = [
        (partner(s_me, k), u_other if flip else u_me)
        for k in range(n_space)
        for flip in (0, 1)
        if k or flip
    ]
    quad_peers = [(f_me, u_other), (f_other, u_me), (f_other, u_other)]

    barrier = pltpu.get_barrier_semaphore()
    for space, sub in meta_peers:
        pl.semaphore_signal(
            barrier,
            inc=1,
            device_id={"space": space, "feat": f_me, "sub": sub},
            device_id_type=MESH,
        )
    for feat, sub in quad_peers[1:]:
        pl.semaphore_signal(
            barrier,
            inc=1,
            device_id={"space": s_me, "feat": feat, "sub": sub},
            device_id_type=MESH,
        )

    fetched["x"].wait()
    fetched["w_embed"].wait()
    grid_full[f_me] = lax.dot_general(
        x_ref[...], w_embed_ref[...], (((0,), (0,)), ((), ())), preferred_element_type=F32
    ).astype(BF16)

    block_count = src_ref.shape[1]
    slot_count = n_space * CAP
    square = (block_count, block_count)
    first = lax.broadcasted_iota(jnp.int32, square, 0)
    second = lax.broadcasted_iota(jnp.int32, square, 1)
    ones = jnp.ones((block_count, LANES), BF16)

    def column(row):
        spread = jnp.where(first == second, jnp.broadcast_to(row.astype(F32), square), 0.0)
        return mm(spread.astype(BF16), ones)

    for t in range(3):
        for name in ("owner", "block", "src", "off"):
            fetched[(name, t)].wait()
        own_row = owner_ref[t]
        own_col = column(own_row)[:, :block_count]
        block_col = column(block_ref[t])
        earlier = jnp.where((own_col == own_row.astype(F32)) & (first < second), 1.0, 0.0)
        rank = jnp.sum(earlier, axis=0, keepdims=True)
        slot_row = own_row.astype(F32) * float(CAP) + rank
        slots = lax.broadcasted_iota(jnp.int32, (slot_count, block_count), 0).astype(F32)
        pick = jnp.where(slots == slot_row, 1.0, 0.0).astype(BF16)
        offs = off_ref[t].astype(F32)
        rows = jnp.where(offs >= 0.0, offs + 128.0 * block_col + 1.0, 0.0).astype(BF16)
        src_slots = mm(pick, src_ref[t].astype(F32).astype(BF16))
        row_slots = mm(pick, rows)
        for o in range(n_space):
            part = slice(o * CAP, (o + 1) * CAP)
            meta_send[o, t] = jnp.concatenate([src_slots[part], row_slots[part]], axis=0).astype(
                BF16
            )
    my_slot = s_me * 2 + u_me
    meta_buf[my_slot] = meta_send[s_me]

    pl.semaphore_wait(barrier, len(meta_peers) + 2)

    def feat_copy(index, src, dst):
        return remote(src, dst, feat_ss.at[index], feat_rs.at[index], feat=f_other)

    def feat_push(index, src, dst):
        copy = feat_copy(index, src, dst)
        copy.start()
        sends.append(copy)

    def sib_copy(index, ref):
        return remote(ref, ref, sib_ss.at[index], sib_rs.at[index], sub=u_other)

    def relay(index, arrived):
        feat_copy(index, arrived, arrived).wait_recv()
        copy = sib_copy(index, arrived)
        copy.start()
        sends.append(copy)

    feat_push(0, grid_full.at[f_me, my_rows], grid_full.at[f_me, my_rows])
    for i, (space, sub) in enumerate(meta_peers):
        push(
            meta_send.at[space],
            meta_buf.at[my_slot],
            meta_ss.at[i],
            meta_rs.at[my_slot],
            space=space,
            sub=sub,
        )
    feat_push(1, mesh_hbm.at[my_rows], mesh_full.at[f_me, my_rows])
    feat_push(2, w_out_hbm.at[0, my_wout], wout_peer.at[0, my_wout])

    fetched["bias"].wait()
    for t in range(3):
        row = bias_ref[t : t + 1, :]
        bias_buf[t] = jnp.transpose(jnp.broadcast_to(row, (LANES, LANES)))

    def project(latents, weight_ref, t):
        width = latents.shape[2]
        total = mm(latents[0], weight_ref[t, 0:width, :])
        total += mm(latents[1], weight_ref[t, width : 2 * width, :])
        return jnp.transpose(total).astype(BF16)

    def start_ps(latents, t):
        ps_buf[t, s_me] = project(latents, w_send_ref, t)
        for k in range(1, n_space):
            push(
                ps_buf.at[t, s_me],
                ps_buf.at[t, s_me],
                ps_ss.at[t, k],
                ps_rs.at[t, s_me],
                space=partner(s_me, k),
            )

    def build_hots(t):
        node = lax.broadcasted_iota(jnp.int32, (rows_count, LANES), 0).astype(F32)

        def body(i, carry):
            meta = meta_buf[i, t].astype(F32)
            for j in range(CAP):
                lanes = slice((j % CHUNK) * LANES, (j % CHUNK + 1) * LANES)
                place = i * (CAP // CHUNK) + j // CHUNK
                hots[t, place, 0:rows_count, lanes] = jnp.where(
                    node == meta[j : j + 1], 1.0, 0.0
                ).astype(BF16)
                hots[t, place, rows_count : 2 * rows_count, lanes] = jnp.where(
                    node + 1.0 == meta[CAP + j : CAP + j + 1], 1.0, 0.0
                ).astype(BF16)
            return carry

        lax.fori_loop(0, 2 * n_space, body, 0)

    def edges(t):
        per_space = 2 * CAP // CHUNK
        recv_table = pr_buf[t]
        bias = jnp.concatenate([bias_buf[t]] * CHUNK, axis=1)
        total = jnp.zeros((rows_count, LANES), F32)
        for k in range(n_space):
            space = partner(s_me, k)
            if k:
                remote(
                    ps_buf.at[t, space],
                    ps_buf.at[t, space],
                    ps_ss.at[t, k],
                    ps_rs.at[t, space],
                    space=space,
                ).wait_recv()
            send_table = ps_buf[t, space]

            def body(c, acc, send_table=send_table, space=space):
                place = space * per_space + c
                send_hot = hots[t, place, 0:rows_count, :]
                recv_hot = hots[t, place, rows_count : 2 * rows_count, :]
                half = 0.5 * (mm(send_table, send_hot) + mm(recv_table, recv_hot) + bias)
                hidden = (half + half * jnp.tanh(half)).astype(BF16)
                return acc + lax.dot_general(
                    recv_hot, hidden, (((1,), (1,)), ((), ())), preferred_element_type=F32
                )

            total = lax.fori_loop(0, per_space, body, total, unroll=True)
        return total

    q_me = f_me * 2 + u_me

    def start_agg(t, total):
        agg_buf[t, q_me] = total.astype(BF16)
        for i, (feat, sub) in enumerate(quad_peers):
            push(
                agg_buf.at[t, q_me],
                agg_buf.at[t, q_me],
                agg_ss.at[t, i],
                agg_rs.at[t, q_me],
                feat=feat,
                sub=sub,
            )

    def wait_agg(t):
        for i, (feat, sub) in enumerate(quad_peers):
            q = feat * 2 + sub
            remote(
                agg_buf.at[t, q],
                agg_buf.at[t, q],
                agg_ss.at[t, i],
                agg_rs.at[t, q],
                feat=feat,
                sub=sub,
            ).wait_recv()
        own = jnp.concatenate([agg_buf[t, f_me * 2], agg_buf[t, f_me * 2 + 1]], axis=1)
        other = jnp.concatenate([agg_buf[t, f_other * 2], agg_buf[t, f_other * 2 + 1]], axis=1)
        return own, other

    def advance(base, t, to):
        own, other = wait_agg(t)
        sib_copy(2 + t, wout_peer.at[t, sib_wout]).wait_recv()
        if t == 0:
            fetched["w_out"].wait()
        width = base.shape[2]
        for f in range(2):
            cols = slice(f * width, (f + 1) * width)
            update = mm(own, w_out_ref[t, :, cols]) + mm(other, wout_peer[t, :, cols])
            latent[to, f] = (base[f].astype(F32) + update).astype(BF16)

    for i, (space, sub) in enumerate(meta_peers):
        slot = space * 2 + sub
        remote(
            meta_send.at[space],
            meta_buf.at[slot],
            meta_ss.at[i],
            meta_rs.at[slot],
            space=space,
            sub=sub,
        ).wait_recv()
    relay(0, grid_full.at[f_other, my_rows])
    fetched["w_send"].wait()
    sib_copy(0, grid_full.at[f_other, sib_rows]).wait_recv()
    start_ps(grid_full, 0)
    relay(1, mesh_full.at[f_other, my_rows])
    build_hots(0)
    fetched["w_recv"].wait()
    fetched["mesh"].wait()
    sib_copy(1, mesh_full.at[f_other, sib_rows]).wait_recv()
    pr_buf[0] = project(mesh_full, w_recv_ref, 0)
    start_agg(0, edges(0))
    their_cols = pl.ds(pl.multiple_of(f_other * half_width, LANES), half_width)
    my_cols = pl.ds(pl.multiple_of(f_me * half_width, LANES), half_width)
    feat_push(3, w_out_hbm.at[1, my_wout], wout_peer.at[1, my_wout])
    feat_push(4, w_out_hbm.at[2, my_wout, their_cols], wout_last.at[my_wout])
    relay(2, wout_peer.at[0, my_wout])
    build_hots(1)
    advance(mesh_full, 0, 0)

    start_ps(latent.at[0], 1)
    pr_buf[1] = project(latent.at[0], w_recv_ref, 1)
    pr_buf[2] = project(grid_full, w_recv_ref, 2)
    start_agg(1, edges(1))
    relay(3, wout_peer.at[1, my_wout])
    relay(4, wout_last.at[my_wout])
    build_hots(2)
    advance(latent.at[0], 1, 1)

    start_ps(latent.at[1], 2)
    start_agg(2, edges(2))
    own, other = wait_agg(2)
    sib_copy(4, wout_last.at[sib_wout]).wait_recv()
    update = mm(own, w_out_ref[2, :, my_cols]) + mm(other, wout_last[...])
    out_ref[...] = (grid_full[f_me].astype(F32) + update).astype(BF16)
    for copy in sends:
        copy.wait_send()


def fused_on_device(
    n_space,
    x_grid,
    mesh_nodes,
    w_embed,
    w_send,
    w_recv,
    w_out,
    edge_bias,
    enc_sources,
    enc_owners,
    enc_blocks,
    enc_offsets,
    proc_sources,
    proc_owners,
    proc_blocks,
    proc_offsets,
    dec_sources,
    dec_owners,
    dec_blocks,
    dec_offsets,
):
    rows, half = mesh_nodes.shape
    lat = w_out.shape[2]
    blocks = enc_sources.shape[0]
    hbm = pl.BlockSpec(memory_space=pl.ANY)
    chunks = n_space * 2 * CAP // CHUNK
    dma = pltpu.SemaphoreType.DMA
    return pl.pallas_call(
        functools.partial(fused_kernel, n_space),
        out_shape=jax.ShapeDtypeStruct((rows, half), BF16),
        in_specs=[hbm] * 19,
        out_specs=pl.BlockSpec(memory_space=pltpu.VMEM),
        scratch_shapes=[
            pltpu.VMEM((x_grid.shape[1], rows), BF16),
            pltpu.VMEM(w_embed.shape, BF16),
            pltpu.VMEM((3, lat, LANES), BF16),
            pltpu.VMEM((3, lat, LANES), BF16),
            pltpu.VMEM(w_out.shape, BF16),
            pltpu.VMEM((3, LANES), F32),
            pltpu.VMEM((3, blocks, LANES), jnp.int32),
            pltpu.VMEM((3, blocks, LANES), jnp.int32),
            pltpu.VMEM((3, 1, blocks), jnp.int32),
            pltpu.VMEM((3, 1, blocks), jnp.int32),
            dma((19,)),
            dma((5,)),
            dma((5,)),
            pltpu.VMEM((2, rows, half), BF16),
            pltpu.VMEM((2, rows, half), BF16),
            pltpu.VMEM((2, 2, rows, half), BF16),
            pltpu.VMEM((n_space, 3, 2 * CAP, LANES), BF16),
            pltpu.VMEM((2 * n_space, 3, 2 * CAP, LANES), BF16),
            pltpu.VMEM((3, n_space, LANES, rows), BF16),
            pltpu.VMEM((3, LANES, rows), BF16),
            pltpu.VMEM((3, 4, rows, LANES), BF16),
            pltpu.VMEM((2, half, lat), BF16),
            pltpu.VMEM((half, half), BF16),
            pltpu.VMEM((3, LANES, LANES), F32),
            pltpu.VMEM((3, chunks, 2 * rows, CHUNK * LANES), BF16),
            dma((2 * n_space,)),
            dma((2 * n_space,)),
            dma((5,)),
            dma((5,)),
            dma((3, n_space)),
            dma((3, n_space)),
            dma((3, 3)),
            dma((3, 4)),
        ],
        compiler_params=pltpu.CompilerParams(
            collective_id=0, has_side_effects=True, vmem_limit_bytes=52 * 1024 * 1024
        ),
    )(
        x_grid.T,
        mesh_nodes,
        w_embed,
        w_send,
        w_recv,
        w_out,
        edge_bias,
        enc_owners.reshape(1, blocks),
        enc_blocks.reshape(1, blocks),
        enc_sources,
        enc_offsets,
        proc_owners.reshape(1, blocks),
        proc_blocks.reshape(1, blocks),
        proc_sources,
        proc_offsets,
        dec_owners.reshape(1, blocks),
        dec_blocks.reshape(1, blocks),
        dec_sources,
        dec_offsets,
    )


def solution(mesh):
    in_specs = (
        P(("groups", "space"), None),
        P("space", "feat"),
        P(None, "feat"),
        P(None, None, "feat"),
        P(None, None, "feat"),
        P(None, "feat", None),
        P(None, "feat"),
        P(("space", "sub"), None),
        P(("space", "sub"), None),
        P(("space", "sub")),
        P(("space", "sub"), None),
        P(("space", "sub"), None),
        P(("space", "sub"), None),
        P(("space", "sub")),
        P(("space", "sub"), None),
        P(("space", "sub"), None),
        P(("space", "sub"), None),
        P(("space", "sub")),
        P(("space", "sub"), None),
    )
    out_specs = P(("groups", "space"), "feat")
    run = on_device
    if fits_kernel(mesh):
        run = functools.partial(fused_on_device, mesh.shape["space"])
    return jax.shard_map(
        run, mesh=mesh, in_specs=in_specs, out_specs=out_specs, check_vma=False
    )
```
